32 devices in a mesh: replica: 16 (over z, y, core), shard: 2 (over x).
Axes of the slice: x: 2, y: 2, z: 4, core: 2. Of those that a mesh axis runs over, the one named last changes fastest.
Arguments:
- tokens_in: bfloat16 [64, 256, 384], P('replica', 'shard'), may hold values from -6 to 6
- condition: bfloat16 [64, 384], P('replica'), may hold values from -6 to 6
- cotangent: bfloat16 [64, 256, 384], P('replica', 'shard'), may hold values from -6 to 6
- modulate_weight: bfloat16 [384, 2304], P('shard'), may hold values from -0.3125 to 0.3125
- modulate_bias: bfloat16 [2304], P('shard'), may hold values from -3 to 3
- attend_weight: bfloat16 [384, 1152], P('shard'), may hold values from -0.3125 to 0.3125
- query_value_bias: bfloat16 [768], P('shard'), may hold values from -3 to 3
- output_weight: bfloat16 [384, 384], P('shard'), may hold values from -2.5 to 2.5
- output_bias: bfloat16 [384], P('shard'), may hold values from -3 to 3
- widening_weight: bfloat16 [384, 1536], P('shard'), may hold values from -0.3125 to 0.3125
- widening_bias: bfloat16 [1536], P('shard'), may hold values from -3 to 3
- narrowing_weight: bfloat16 [1536, 384], P('shard'), may hold values from -0.15625 to 0.15625
- narrowing_bias: bfloat16 [384], P('shard'), may hold values from -3 to 3
Outputs:
- tokens_out: bfloat16 [64, 256, 384], P('replica', 'shard')
- grad_tokens: float32 [64, 256, 384], P('replica', 'shard')
- grad_condition: float32 [64, 384], P('replica')
- grad_modulate_weight: float32 [384, 2304], P('shard')
- grad_modulate_bias: float32 [2304], P('shard')
- grad_attend_weight: float32 [384, 1152], P('shard')
- grad_query_value_bias: float32 [768], P('shard')
- grad_output_weight: float32 [384, 384], P('shard')
- grad_output_bias: float32 [384], P('shard')
- grad_expand_weight: float32 [384, 1536], P('shard')
- grad_expand_bias: float32 [1536], P('shard')
- grad_shrink_weight: float32 [1536, 384], P('shard')
- grad_shrink_bias: float32 [384], P('shard')
The draws below stay inside these ranges and needn't reach their ends.
All inputs are finite; a program needn't handle non-finite values.
Results may differ from the reference program's by a relative error of at most 0.01.
The reference program's roundings to bfloat16 on the way count: a program that leaves them out, or rounds other values in their place, can miss the bound.
Values may be sent and summed in bfloat16 or wider, within the bound.
A program may use at most 128 MiB of HBM per device.

```python
import math
import jax
import jax.numpy as jnp
from jax import lax

D = 384
HEADS = 6
HEAD_DIM = 64
FF = 1536
SEQ = 256
LATENTS = 64


def shard_levels(key, shape, cuts, low, high):
    def one(dim, parts):
        draws = jax.random.uniform(jax.random.fold_in(jax.random.fold_in(key, 6), dim), (parts,), jnp.float32, low / len(cuts), high / len(cuts))
        return jnp.repeat(jnp.exp(draws), shape[dim] // parts).reshape((-1,) + (1,) * (len(shape) - dim - 1))

    loudness = one(*cuts[0])
    for cut in cuts[1:]:
        loudness = loudness * one(*cut)
    return loudness


def centred(rng, extent, scale, bound, split=(), held_as=jnp.bfloat16):
    values = jax.random.normal(rng, extent, jnp.float32) * scale
    if len(split) > 0:
        values = shard_levels(rng, extent, split, -0.22, 0.18) * values
    return jnp.clip(values, min=-bound, max=bound).astype(held_as)


def setup_inputs(seed: int = 0) -> dict:
    streams_of = jax.random.split(jax.random.key(seed), 14)
    tokens_in = centred(streams_of[0], (LATENTS, SEQ, D), 1.0, 6.0, ((0, 16), (1, 2)))
    condition = centred(streams_of[1], (LATENTS, D), 1.0, 6.0, ((0, 16),))
    cotangent = centred(streams_of[2], (LATENTS, SEQ, D), 1.0, 6.0, ((0, 16), (1, 2)))
    modulate_weight = centred(streams_of[3], (D, 6 * D), D ** -0.5, 0.3125, ((0, 2),))
    modulate_bias = centred(streams_of[4], (6 * D,), 0.5, 3.0, ((0, 2),))
    attend_weight = centred(streams_of[5], (D, 3 * D), D ** -0.5, 0.3125, ((0, 2),))
    query_value_bias = centred(streams_of[6], (2 * D,), 0.5, 3.0, ((0, 2),))
    output_weight = centred(streams_of[7], (D, D), (D // 64) ** -0.5, 2.5, ((0, 2),))
    output_bias = centred(streams_of[8], (D,), 0.5, 3.0, ((0, 2),))
    widening_weight = centred(streams_of[9], (D, FF), D ** -0.5, 0.3125, ((0, 2),))
    widening_bias = centred(streams_of[10], (FF,), 0.5, 3.0, ((0, 2),))
    narrowing_weight = centred(streams_of[11], (FF, D), FF ** -0.5, 0.15625, ((0, 2),))
    narrowing_bias = centred(streams_of[12], (D,), 0.5, 3.0, ((0, 2),))
    return dict(tokens_in=tokens_in, condition=condition, cotangent=cotangent, modulate_weight=modulate_weight, modulate_bias=modulate_bias, attend_weight=attend_weight, query_value_bias=query_value_bias, output_weight=output_weight, output_bias=output_bias, widening_weight=widening_weight, widening_bias=widening_bias, narrowing_weight=narrowing_weight, narrowing_bias=narrowing_bias)


exact_arithmetic_flag = lax.Precision.HIGHEST

@jax.custom_vjp
def low(v):
    return lax.optimization_barrier(v.astype(jnp.bfloat16)).astype(jnp.float32)

@jax.custom_vjp
def reduced_precision_backward(v):
    return v

def low_keep(v):
    return (low(v), None)

def low_pass(kept, grad):
    return (grad,)

def back_keep(v):
    return (v, None)

def back_low(kept, grad):
    return (low(grad),)
low.defvjp(low_keep, low_pass)
reduced_precision_backward.defvjp(back_keep, back_low)

def modulate_norm(values, shift, scale):
    average = lax.optimization_barrier(jnp.mean(values, axis=-1, keepdims=True))
    centered = values - average
    variance = lax.optimization_barrier(jnp.mean(centered * centered, axis=-1, keepdims=True))
    return centered * lax.rsqrt(variance + 1e-06) * (1.0 + scale) + shift

def block_forward(tokens, condition, modulate_weight, modulate_bias, attend_weight, query_value_bias, output_weight, output_bias, widening_weight, widening_bias, narrowing_weight, narrowing_bias):
    latents = tokens.shape[0]
    score_scale = HEAD_DIM ** (-0.5)
    cond_act = low(jax.nn.silu(condition))
    modulation = reduced_precision_backward(jnp.dot(cond_act, modulate_weight, precision=exact_arithmetic_flag) + modulate_bias)
    shift_one = modulation[:, None, 0:D]
    scale_one = modulation[:, None, D:2 * D]
    gate_one = modulation[:, None, 2 * D:3 * D]
    shift_two = modulation[:, None, 3 * D:4 * D]
    scale_two = modulation[:, None, 4 * D:5 * D]
    gate_two = modulation[:, None, 5 * D:6 * D]
    normed_one = low(modulate_norm(tokens, shift_one, scale_one))
    zero_bias = jnp.zeros((D,), jnp.float32)
    full_bias = jnp.concatenate([query_value_bias[:D], zero_bias, query_value_bias[D:]])
    projected = low(reduced_precision_backward(jnp.einsum('lsd,de->lse', normed_one, attend_weight, precision=exact_arithmetic_flag) + full_bias))
    queries = projected[..., :D].reshape(latents, SEQ, HEADS, HEAD_DIM)
    keys = projected[..., D:2 * D].reshape(latents, SEQ, HEADS, HEAD_DIM)
    values = projected[..., 2 * D:].reshape(latents, SEQ, HEADS, HEAD_DIM)
    scores = reduced_precision_backward(jnp.einsum('lqhd,lkhd->lhqk', queries, keys, precision=exact_arithmetic_flag) * score_scale)
    highest = lax.optimization_barrier(jnp.max(scores, axis=-1, keepdims=True))
    expo = jnp.exp(scores - highest)
    probs = low(expo / lax.optimization_barrier(jnp.sum(expo, axis=-1, keepdims=True)))
    attended = jnp.einsum('lhqk,lkhd->lqhd', probs, values, precision=exact_arithmetic_flag).reshape(latents, SEQ, D)
    attended = low(reduced_precision_backward(attended))
    attn_out = reduced_precision_backward(jnp.einsum('lsd,de->lse', attended, output_weight, precision=exact_arithmetic_flag) + output_bias)
    middle = tokens + gate_one * attn_out
    second_normalized = low(modulate_norm(middle, shift_two, scale_two))
    hidden_preactivation = reduced_precision_backward(jnp.einsum('bei,ig->beg', second_normalized, widening_weight, precision=exact_arithmetic_flag) + widening_bias)
    hidden_activation = low(jax.nn.gelu(hidden_preactivation, approximate=True))
    feedforward_output = reduced_precision_backward(jnp.einsum('ega,ap->egp', hidden_activation, narrowing_weight, precision=exact_arithmetic_flag) + narrowing_bias)
    return middle + gate_two * feedforward_output

def reference(tokens_in, condition, cotangent, modulate_weight, modulate_bias, attend_weight, query_value_bias, output_weight, output_bias, widening_weight, widening_bias, narrowing_weight, narrowing_bias):
    weight_list = [item.astype(jnp.float32) for item in (modulate_weight, modulate_bias, attend_weight, query_value_bias, output_weight, output_bias, widening_weight, widening_bias, narrowing_weight, narrowing_bias)]
    latents = tokens_in.shape[0]
    group = math.gcd(latents, max(1, 4096 // SEQ))
    rounds = latents // group
    tokens_all = tokens_in.astype(jnp.float32).reshape(rounds, group, SEQ, D)
    cond_all = condition.astype(jnp.float32).reshape(rounds, group, D)
    upstream_all = cotangent.astype(jnp.float32).reshape(rounds, group, SEQ, D)

    def one_round(totals, inputs):
        tokens_grp, cond_grp, upstream_grp = inputs
        output, pullback = jax.vjp(block_forward, tokens_grp, cond_grp, *weight_list)
        grads = pullback(upstream_grp)
        totals = tuple((running + update for running, update in zip(totals, grads[2:])))
        return (totals, (output.astype(jnp.bfloat16), grads[0], grads[1]))
    initial = tuple((jnp.zeros(item.shape, jnp.float32) for item in weight_list))
    totals, (outputs, grad_tok, grad_cnd) = lax.scan(one_round, initial, (tokens_all, cond_all, upstream_all))
    return (outputs.reshape(latents, SEQ, D), grad_tok.reshape(latents, SEQ, D), grad_cnd.reshape(latents, D), totals[0], totals[1], totals[2], totals[3], totals[4], totals[5], totals[6], totals[7], totals[8], totals[9])
```

```python
import functools
import jax
import jax.numpy as jnp
from jax import lax
from jax.experimental import pallas as pl
from jax.experimental.pallas import tpu as pltpu
from jax.sharding import PartitionSpec as P

D = 384
HEADS = 6
HEAD_DIM = 64
FF = 1536
CHUNKS = 3
ROWS = 768
BLOCK_ROWS = 80
F32 = jnp.float32
BF16 = jnp.bfloat16
SWAP = [(0, 1), (1, 0)]


def modulate_norm(values, shift, scale):
    average = jnp.mean(values, axis=-1, keepdims=True)
    centered = values - average
    variance = jnp.mean(centered * centered, axis=-1, keepdims=True)
    return centered * lax.rsqrt(variance + 1e-06) * (1.0 + scale) + shift


def gelu_tanh(values):
    return jax.nn.gelu(values, approximate=True)


def flip(index, bit):
    step = 1 << bit
    return index + step - 2 * step * ((index // step) % 2)


def bit_of(index, bit):
    return (index // (1 << bit)) % 2


def greet(partners):
    barrier = pltpu.get_barrier_semaphore()
    for partner in partners:
        pl.semaphore_signal(barrier, inc=1, device_id=partner, device_id_type=pl.DeviceIdType.MESH)
    pl.semaphore_wait(barrier, len(partners))


def gather_kernel(
    tok, cot, small, wa, wo, ww, wn,
    tok_all, cot_all, small_other, wa_all, wo_all, ww_all, wn_all,
    send_one, recv_one, send_w, recv_w, local_sem,
):
    r, s = lax.axis_index("replica"), lax.axis_index("shard")
    o = 1 - s
    over_x, over_core, over_y = (r, o), (flip(r, 0), s), (flip(r, 1), s)
    greet((over_x, over_core, over_y))

    def remote(src, dst, send, recv, device):
        copy = pltpu.make_async_remote_copy(
            src_ref=src, dst_ref=dst, send_sem=send, recv_sem=recv,
            device_id=device, device_id_type=pl.DeviceIdType.MESH,
        )
        return copy

    length = tok.shape[1]
    group = tok.shape[0] // 2
    place = pl.ds(pl.multiple_of(s * length, length), length)

    def exchange(src, dst, k):
        return remote(
            src.at[pl.ds(o * group, group)], dst.at[:, place], send_one.at[k], recv_one.at[k], over_x
        )

    swaps = [
        remote(small, small_other, send_one.at[0], recv_one.at[0], over_x),
        exchange(tok, tok_all, 1),
        exchange(cot, cot_all, 2),
    ]
    swaps[0].start()
    swaps[1].start()

    pairs = ((wa, wa_all), (wo, wo_all), (ww, ww_all), (wn, wn_all))
    quarter = r % 4

    def rows_at(full, half, q):
        n = full.shape[0] // 8
        return full.at[pl.ds(pl.multiple_of(half * (4 * n) + q * n, n), n)]

    first = []
    for k, (own, full) in enumerate(pairs):
        n = own.shape[0] // 4
        c = remote(
            own.at[pl.ds(pl.multiple_of(quarter * n, n), n)], rows_at(full, s, quarter),
            send_w.at[k, 0], recv_w.at[k, 0], over_x,
        )
        c.start()
        first.append(c)
    swaps[2].start()
    locals_ = []
    for k, (src, dst) in enumerate(((tok, tok_all), (cot, cot_all))):
        locals_.append(
            pltpu.make_async_copy(src.at[pl.ds(s * group, group)], dst.at[:, place], local_sem.at[k])
        )
    for k, (own, full) in enumerate(pairs):
        n = own.shape[0]
        locals_.append(
            pltpu.make_async_copy(own, full.at[pl.ds(pl.multiple_of(s * n, n), n)], local_sem.at[2 + k])
        )
    for c in locals_:
        c.start()
    later = []
    for k, (own, full) in enumerate(pairs):
        first[k].wait_recv()
        mine = rows_at(full, o, quarter)
        by_y = remote(mine, mine, send_w.at[k, 1], recv_w.at[k, 1], over_y)
        by_y.start()
        by_core = remote(mine, mine, send_w.at[k, 2], recv_w.at[k, 2], over_core)
        by_core.start()
        later.append((by_y, by_core))
    last = []
    for k, (own, full) in enumerate(pairs):
        later[k][0].wait_recv()
        came = rows_at(full, o, flip(quarter, 1))
        c = remote(came, came, send_w.at[k, 3], recv_w.at[k, 3], over_core)
        c.start()
        last.append(c)
    for k in range(4):
        later[k][1].wait_recv()
        last[k].wait_recv()
    for c in swaps:
        c.wait_recv()
    for c in locals_:
        c.wait()
    for c in swaps + first + last:
        c.wait_send()
    for a, b in later:
        a.wait_send()
        b.wait_send()


def gather_all(tok, cot, small, wa, wo, ww, wn):
    any_spec = pl.BlockSpec(memory_space=pl.ANY)
    group = tok.shape[0] // 2

    def full(w):
        return jax.ShapeDtypeStruct((w.shape[0] * 2, w.shape[1]), w.dtype)

    tokens = jax.ShapeDtypeStruct((group, 2 * tok.shape[1], D), BF16)
    return pl.pallas_call(
        gather_kernel,
        out_shape=(
            tokens, tokens, jax.ShapeDtypeStruct(small.shape, small.dtype),
            full(wa), full(wo), full(ww), full(wn),
        ),
        in_specs=[any_spec] * 7,
        out_specs=(any_spec,) * 7,
        scratch_shapes=[
            pltpu.SemaphoreType.DMA((3,)),
            pltpu.SemaphoreType.DMA((3,)),
            pltpu.SemaphoreType.DMA((4, 4)),
            pltpu.SemaphoreType.DMA((4, 4)),
            pltpu.SemaphoreType.DMA((6,)),
        ],
        compiler_params=pltpu.CompilerParams(collective_id=0, has_side_effects=True),
    )(tok, cot, small, wa, wo, ww, wn)


def reduce_kernel(
    bits, grads, block, out, blocks,
    core_in, x_out, x_in, total, half_out, half_in, extra_out, extra_in,
    send_sem, recv_sem, send_blk, recv_blk, local_sem,
):
    r, s = lax.axis_index("replica"), lax.axis_index("shard")
    o = 1 - s
    over_x = (r, o)
    over = [(flip(r, k), s) for k in range(bits)]
    greet([over_x] + over)
    core = bit_of(r, 0)

    def remote(src, dst, send, recv, device):
        copy = pltpu.make_async_remote_copy(
            src_ref=src, dst_ref=dst, send_sem=send, recv_sem=recv,
            device_id=device, device_id_type=pl.DeviceIdType.MESH,
        )
        copy.start()
        return copy

    pending = []

    order = [(over[k], bit_of(r, k)) for k in range(bits - 1, 0, -1)]
    order += [(over_x, s), (over[0], core)]
    index = sum(b * (1 << k) for k, (_, b) in enumerate(order))
    own_block = pltpu.make_async_copy(block, blocks.at[index], local_sem)
    own_block.start()

    def gather_steps():
        own_block.wait()
        for k, (device, _) in enumerate(order):
            count = 1 << k
            start = (index // count) * count
            part = blocks.at[pl.ds(start, count)]
            c = remote(part, part, send_blk.at[k], recv_blk.at[k], device)
            pending.append(c)
            yield
            c.wait_recv()

    def rows(n, start):
        return pl.ds(pl.multiple_of(start, 16), n)

    def chunk_steps(j):
        base = j * ROWS
        half = ROWS // 2
        away = rows(half, base + (1 - core) * half)
        kept = rows(half, base + core * half)
        c = remote(grads.at[:, away], core_in.at[j], send_sem.at[j, 0], recv_sem.at[j, 0], over[0])
        pending.append(c)
        yield
        c.wait_recv()
        x_out[j] = (grads[o, kept].astype(F32) + core_in[j, o].astype(F32)).astype(BF16)
        c = remote(x_out.at[j], x_in.at[j], send_sem.at[j, 1], recv_sem.at[j, 1], over_x)
        pending.append(c)
        total[j] = grads[s, kept].astype(F32) + core_in[j, s].astype(F32)
        yield
        c.wait_recv()
        total[j] += x_in[j].astype(F32)
        n, start, at = half // 2, 0, 0
        for k in (1, 2, 3):
            b = bit_of(r, k)
            spot = rows(n, at)
            half_out[j, spot] = total[j, rows(n, start + (1 - b) * n)].astype(BF16)
            c = remote(
                half_out.at[j, spot], half_in.at[j, spot],
                send_sem.at[j, 1 + k], recv_sem.at[j, 1 + k], over[k],
            )
            pending.append(c)
            yield
            c.wait_recv()
            start = start + b * n
            total[j, rows(n, start)] += half_in[j, spot].astype(F32)
            at += n
            n //= 2
        n *= 2
        for e in range(bits - 4):
            extra_out[j, e] = total[j, rows(n, start)].astype(BF16)
            c = remote(
                extra_out.at[j, e], extra_in.at[j, e],
                send_sem.at[j, 9 + e], recv_sem.at[j, 9 + e], over[4 + e],
            )
            pending.append(c)
            yield
            c.wait_recv()
            total[j, rows(n, start)] += extra_in[j, e].astype(F32)
        spot = base + core * half + start
        out[rows(n, spot)] = total[j, rows(n, start)].astype(BF16)
        for step, k in enumerate((3, 2, 1, 0)):
            part = out.at[rows(n, spot)]
            c = remote(part, part, send_sem.at[j, 5 + step], recv_sem.at[j, 5 + step], over[k])
            pending.append(c)
            yield
            c.wait_recv()
            spot = spot - bit_of(r, k) * n
            n *= 2

    waiting = [chunk_steps(j) for j in range(CHUNKS)]
    running = [gather_steps()]
    while running or waiting:
        if waiting:
            running.append(waiting.pop(0))
        for steps in list(running):
            if next(steps, 0) == 0:
                running.remove(steps)
    for c in pending:
        c.wait_send()


def reduce_all(grads, block, replicas):
    bits = replicas.bit_length() - 1
    extra = max(bits - 4, 1)
    vmem = pl.BlockSpec(memory_space=pltpu.VMEM)
    half = ROWS // 2
    return pl.pallas_call(
        functools.partial(reduce_kernel, bits),
        out_shape=(
            jax.ShapeDtypeStruct((CHUNKS * ROWS, D), BF16),
            jax.ShapeDtypeStruct((2 * replicas, BLOCK_ROWS, 128), BF16),
        ),
        in_specs=[vmem, vmem],
        out_specs=(vmem, vmem),
        scratch_shapes=[
            pltpu.VMEM((CHUNKS, 2, half, D), BF16),
            pltpu.VMEM((CHUNKS, half, D), BF16),
            pltpu.VMEM((CHUNKS, half, D), BF16),
            pltpu.VMEM((CHUNKS, half, D), F32),
            pltpu.VMEM((CHUNKS, half, D), BF16),
            pltpu.VMEM((CHUNKS, half, D), BF16),
            pltpu.VMEM((CHUNKS, extra, half // 8, D), BF16),
            pltpu.VMEM((CHUNKS, extra, half // 8, D), BF16),
            pltpu.SemaphoreType.DMA((CHUNKS, 9 + extra)),
            pltpu.SemaphoreType.DMA((CHUNKS, 9 + extra)),
            pltpu.SemaphoreType.DMA((bits + 1,)),
            pltpu.SemaphoreType.DMA((bits + 1,)),
            pltpu.SemaphoreType.DMA,
        ],
        compiler_params=pltpu.CompilerParams(
            collective_id=1, has_side_effects=True, vmem_limit_bytes=48 * 2**20
        ),
    )(grads, block)


def in_halves(gradient):
    rows = gradient.shape[0] // 2
    columns = [gradient[:, i : i + D].reshape(2, rows, D) for i in range(0, gradient.shape[1], D)]
    return jnp.concatenate(columns, axis=1) if len(columns) > 1 else columns[0]


def on_device(
    tokens_in,
    condition,
    cotangent,
    modulate_weight,
    modulate_bias,
    attend_weight,
    query_value_bias,
    output_weight,
    output_bias,
    widening_weight,
    widening_bias,
    narrowing_weight,
    narrowing_bias,
):
    rank = lax.axis_index("shard")
    replicas = lax.axis_size("replica")
    score_scale = HEAD_DIM ** (-0.5)
    latents = tokens_in.shape[0] // 2
    local_len = tokens_in.shape[1]
    seq_len = 2 * local_len
    own_rows = D // 2
    cond_float = condition.astype(F32)
    cond_act_all = jax.nn.silu(cond_float).astype(BF16)
    own_act = lax.dynamic_slice_in_dim(cond_act_all, rank * own_rows, own_rows, 1)
    mod_part = jnp.dot(own_act, modulate_weight, preferred_element_type=F32)
    mod_keep = lax.dynamic_slice_in_dim(mod_part, rank * latents, latents, 0)
    mod_send = lax.dynamic_slice_in_dim(mod_part, (1 - rank) * latents, latents, 0)
    biases = jnp.concatenate(
        [modulate_bias, query_value_bias, output_bias, widening_bias, narrowing_bias]
    ).astype(F32)
    sent = jnp.concatenate([mod_send.reshape(-1), biases])
    pad = (-sent.shape[0]) % 1024
    small = jnp.pad(sent, (0, pad)).reshape(-1, 128)
    tokens_in, cotangent, small_other, w_attend, w_output, widening_matrix, narrowing_matrix = (
        gather_all(
            tokens_in, cotangent, small, attend_weight, output_weight, widening_weight, narrowing_weight
        )
    )
    small_other = small_other.reshape(-1)
    count = latents * 6 * D
    mod_other = small_other[:count].reshape(latents, 6 * D)
    bias_other = small_other[count : count + biases.shape[0]]

    def both(start, size):
        own, other = biases[start : start + size], bias_other[start : start + size]
        return jnp.where(
            rank == 0, jnp.concatenate([own, other]), jnp.concatenate([other, own])
        )

    b_modulate = both(0, 3 * D)
    b_query_value = both(3 * D, D)
    b_output = both(4 * D, D // 2)
    b_expand = both(4 * D + D // 2, FF // 2)
    b_shrink = both(4 * D + D // 2 + FF // 2, D // 2)

    tokens_float = tokens_in.astype(F32)
    modulation = mod_keep + mod_other + b_modulate
    shift_one = modulation[:, None, 0:D]
    scale_one = modulation[:, None, D : 2 * D]
    gate_one = modulation[:, None, 2 * D : 3 * D]
    shift_two = modulation[:, None, 3 * D : 4 * D]
    scale_two = modulation[:, None, 4 * D : 5 * D]
    gate_two = modulation[:, None, 5 * D : 6 * D]
    normed_one = modulate_norm(tokens_float, shift_one, scale_one).astype(BF16)
    full_bias = jnp.concatenate([b_query_value[:D], jnp.zeros((D,), F32), b_query_value[D:]])
    projected = (
        jnp.einsum("lsd,de->lse", normed_one, w_attend, preferred_element_type=F32) + full_bias
    ).astype(BF16)
    query_heads = projected[..., :D].reshape(latents, seq_len, HEADS, HEAD_DIM)
    key_heads = projected[..., D : 2 * D].reshape(latents, seq_len, HEADS, HEAD_DIM)
    value_heads = projected[..., 2 * D :].reshape(latents, seq_len, HEADS, HEAD_DIM)
    scores = (
        jnp.einsum("lqhd,lkhd->lhqk", query_heads, key_heads, preferred_element_type=F32)
        * score_scale
    )
    highest = jnp.max(scores, axis=-1, keepdims=True)
    log_norm = highest + jnp.log(jnp.sum(jnp.exp(scores - highest), axis=-1, keepdims=True))
    probs = jnp.exp(scores - log_norm)
    probs_low = probs.astype(BF16)
    attended = jnp.einsum("lhqk,lkhd->lqhd", probs_low, value_heads, preferred_element_type=F32)
    attended = attended.reshape(latents, seq_len, D).astype(BF16)
    attn_out = jnp.einsum("lsd,de->lse", attended, w_output, preferred_element_type=F32) + b_output
    middle = tokens_float + gate_one * attn_out
    second_normalized = modulate_norm(middle, shift_two, scale_two).astype(BF16)
    hidden_pre = (
        jnp.einsum("bei,ig->beg", second_normalized, widening_matrix, preferred_element_type=F32)
        + b_expand
    )
    hidden_act = gelu_tanh(hidden_pre).astype(BF16)
    mlp_out = (
        jnp.einsum("ega,ap->egp", hidden_act, narrowing_matrix, preferred_element_type=F32) + b_shrink
    )
    tokens_out = (middle + gate_two * mlp_out).astype(BF16)

    upstream = cotangent.astype(F32)
    d_mlp = (gate_two * upstream).astype(BF16)
    d_gate_two = jnp.sum(upstream * mlp_out, axis=1)
    g_shrink_w = jnp.einsum("ukq,ukc->qc", hidden_act, d_mlp, preferred_element_type=F32)
    g_shrink_b = jnp.sum(d_mlp.astype(F32), axis=(0, 1))
    d_act = jnp.einsum("het,jt->hej", d_mlp, narrowing_matrix, preferred_element_type=F32)
    _, gelu_back = jax.vjp(gelu_tanh, hidden_pre)
    d_pre = gelu_back(d_act)[0].astype(BF16)
    g_expand_w = jnp.einsum("mqo,mqz->oz", second_normalized, d_pre, preferred_element_type=F32)
    g_expand_b = jnp.sum(d_pre.astype(F32), axis=(0, 1))
    d_second = jnp.einsum("pkc,ac->pka", d_pre, widening_matrix, preferred_element_type=F32)
    _, norm_back = jax.vjp(modulate_norm, middle, shift_two, scale_two)
    d_mid_norm, d_shift_two, d_scale_two = norm_back(d_second)
    d_middle = upstream + d_mid_norm
    d_attn = (gate_one * d_middle).astype(BF16)
    d_gate_one = jnp.sum(d_middle * attn_out, axis=1)
    g_output_w = jnp.einsum("lsd,lse->de", attended, d_attn, preferred_element_type=F32)
    g_output_b = jnp.sum(d_attn.astype(F32), axis=(0, 1))
    d_attended = jnp.einsum("lse,de->lsd", d_attn, w_output, preferred_element_type=F32)
    d_attended = d_attended.astype(BF16).reshape(latents, seq_len, HEADS, HEAD_DIM)
    d_probs = jnp.einsum("lqhd,lkhd->lhqk", d_attended, value_heads, preferred_element_type=F32)
    delta_sum = jnp.sum(probs * d_probs, axis=-1, keepdims=True)
    d_scores = (probs * (d_probs - delta_sum)).astype(BF16)
    d_values = jnp.einsum("lhqk,lqhd->lkhd", probs_low, d_attended, preferred_element_type=F32)
    d_queries = (
        jnp.einsum("lhqk,lkhd->lqhd", d_scores, key_heads, preferred_element_type=F32) * score_scale
    )
    d_keys = (
        jnp.einsum("lhqk,lqhd->lkhd", d_scores, query_heads, preferred_element_type=F32) * score_scale
    )
    d_projected = jnp.concatenate(
        [t.reshape(latents, seq_len, D) for t in (d_queries, d_keys, d_values)], axis=-1
    ).astype(BF16)
    g_attend_w = jnp.einsum("lsd,lse->de", normed_one, d_projected, preferred_element_type=F32)
    column_sums = jnp.sum(d_projected.astype(F32), axis=(0, 1))
    g_query_value = jnp.concatenate([column_sums[:D], column_sums[2 * D :]])
    d_norm_one = jnp.einsum("lse,de->lsd", d_projected, w_attend, preferred_element_type=F32)
    _, norm_back = jax.vjp(modulate_norm, tokens_float, shift_one, scale_one)
    d_in_norm, d_shift_one, d_scale_one = norm_back(d_norm_one)
    grad_work = d_middle + d_in_norm
    d_modulation = jnp.concatenate(
        [
            d_shift_one[:, 0],
            d_scale_one[:, 0],
            d_gate_one,
            d_shift_two[:, 0],
            d_scale_two[:, 0],
            d_gate_two,
        ],
        axis=-1,
    ).astype(BF16)
    return finish(
        rank, replicas, latents, local_len, cond_float, cond_act_all, modulate_weight, tokens_out,
        grad_work, d_modulation, g_attend_w, g_query_value, g_output_w, g_output_b, g_expand_w,
        g_expand_b, g_shrink_w, g_shrink_b,
    )


def finish(
    rank, replicas, latents, local_len, cond_float, cond_act_all, modulate_weight, tokens_out,
    grad_work, d_modulation, g_attend_w, g_query_value, g_output_w, g_output_b, g_expand_w,
    g_expand_b, g_shrink_w, g_shrink_b,
):
    def in_order(own, other):
        return jnp.where(rank == 0, jnp.concatenate([own, other]), jnp.concatenate([other, own]))

    def give_back(values):
        own = lax.dynamic_slice_in_dim(values, rank * local_len, local_len, 1)
        away = lax.dynamic_slice_in_dim(values, (1 - rank) * local_len, local_len, 1)
        other = lax.ppermute(away.astype(BF16), "shard", SWAP).astype(values.dtype)
        return in_order(own, other)

    grads = jnp.concatenate(
        [in_halves(g.astype(BF16)) for g in (g_shrink_w, g_expand_w, g_attend_w, g_output_w)], axis=1
    )
    own_cond = lax.dynamic_slice_in_dim(cond_act_all, rank * latents, latents, 0)
    bias_all = jnp.concatenate([g_query_value, g_output_b, g_expand_b, g_shrink_b]).astype(BF16)
    flat = jnp.concatenate([d_modulation.reshape(-1), own_cond.reshape(-1), bias_all])
    block = jnp.pad(flat, (0, BLOCK_ROWS * 128 - flat.shape[0])).reshape(BLOCK_ROWS, 128)
    tokens_result = give_back(tokens_out)
    grad_result = give_back(grad_work)
    d_mod_other = lax.ppermute(d_modulation, "shard", SWAP)
    d_cond_part = jnp.einsum(
        "le,de->ld", in_order(d_modulation, d_mod_other), modulate_weight, preferred_element_type=F32
    )
    d_cond_other = lax.ppermute(d_cond_part, "shard", SWAP)
    d_cond = jnp.where(
        rank == 0,
        jnp.concatenate([d_cond_part, d_cond_other], axis=1),
        jnp.concatenate([d_cond_other, d_cond_part], axis=1),
    )
    _, silu_back = jax.vjp(jax.nn.silu, cond_float)
    grad_condition = silu_back(d_cond)[0]

    reduced, blocks = reduce_all(grads, block, replicas)
    flat_blocks = blocks.reshape(2 * replicas, BLOCK_ROWS * 128)
    n_mod, n_cond = latents * 6 * D, latents * D
    d_mod_all = flat_blocks[:, :n_mod].reshape(-1, 6 * D)
    act_all = flat_blocks[:, n_mod : n_mod + n_cond].reshape(-1, D)
    bias_sum = jnp.sum(flat_blocks[:, n_mod + n_cond : n_mod + n_cond + bias_all.shape[0]].astype(F32), axis=0)
    own_act = lax.dynamic_slice_in_dim(act_all, rank * (D // 2), D // 2, 1)
    g_modulate_w = jnp.einsum("lr,le->re", own_act, d_mod_all, preferred_element_type=F32)
    g_modulate_b = jnp.sum(
        lax.dynamic_slice_in_dim(d_mod_all, rank * 3 * D, 3 * D, 1).astype(F32), axis=0
    )

    def own_bias(start, size):
        return lax.dynamic_slice_in_dim(bias_sum, start + rank * (size // 2), size // 2, 0)

    reduced = reduced.astype(F32)
    half = D // 2
    expand = jnp.concatenate([reduced[768 + i * half : 768 + (i + 1) * half] for i in range(4)], axis=1)
    attend = jnp.concatenate([reduced[1536 + i * half : 1536 + (i + 1) * half] for i in range(3)], axis=1)
    return (
        tokens_result,
        grad_result,
        grad_condition,
        g_modulate_w,
        g_modulate_b,
        attend,
        own_bias(0, 2 * D),
        reduced[1536 + 3 * half :],
        own_bias(2 * D, D),
        expand,
        own_bias(3 * D, FF),
        reduced[:768],
        own_bias(3 * D + FF, D),
    )


def solution(mesh):
    specs = (
        P("shard", None),
        P("shard"),
        P("shard", None),
        P("shard"),
        P("shard", None),
        P("shard"),
        P("shard", None),
        P("shard"),
        P("shard", None),
        P("shard"),
    )
    tokens = P("replica", "shard", None)
    return jax.shard_map(
        on_device,
        mesh=mesh,
        in_specs=(tokens, P("replica", None), tokens) + specs,
        out_specs=(tokens, tokens, P("replica", None)) + specs,
        check_vma=False,
    )
```

```python
import functools
import jax
import jax.numpy as jnp
from jax import lax
from jax.experimental import pallas as pl
from jax.experimental.pallas import tpu as pltpu
from jax.sharding import PartitionSpec as P

D = 384
HEADS = 6
HEAD_DIM = 64
FF = 1536
CHUNKS = 3
ROWS = 768
BLOCK_ROWS = 80
F32 = jnp.float32
BF16 = jnp.bfloat16
SWAP = [(0, 1), (1, 0)]


def flip(index, bit):
    step = 1 << bit
    return index + step - 2 * step * ((index // step) % 2)


def bit_of(index, bit):
    return (index // (1 << bit)) % 2


def greet(partners):
    barrier = pltpu.get_barrier_semaphore()
    for partner in partners:
        pl.semaphore_signal(barrier, inc=1, device_id=partner, device_id_type=pl.DeviceIdType.MESH)
    pl.semaphore_wait(barrier, len(partners))


def gather_kernel(
    tok, cot, small, wa, wo, ww, wn,
    tok_all, cot_all, small_other, wa_all, wo_all, ww_all, wn_all,
    send_one, recv_one, send_w, recv_w, local_sem,
):
    r, s = lax.axis_index("replica"), lax.axis_index("shard")
    o = 1 - s
    over_x, over_core, over_y = (r, o), (flip(r, 0), s), (flip(r, 1), s)
    greet((over_x, over_core, over_y))

    def remote(src, dst, send, recv, device):
        copy = pltpu.make_async_remote_copy(
            src_ref=src, dst_ref=dst, send_sem=send, recv_sem=recv,
            device_id=device, device_id_type=pl.DeviceIdType.MESH,
        )
        return copy

    length = tok.shape[1]
    group = tok.shape[0] // 2
    place = pl.ds(pl.multiple_of(s * length, length), length)

    def exchange(src, dst, k):
        return remote(
            src.at[pl.ds(o * group, group)], dst.at[:, place], send_one.at[k], recv_one.at[k], over_x
        )

    swaps = [
        remote(small, small_other, send_one.at[0], recv_one.at[0], over_x),
        exchange(tok, tok_all, 1),
        exchange(cot, cot_all, 2),
    ]
    swaps[0].start()
    swaps[1].start()

    pairs = ((wa, wa_all), (wo, wo_all), (ww, ww_all), (wn, wn_all))
    quarter = r % 4

    def rows_at(full, half, q):
        n = full.shape[0] // 8
        return full.at[pl.ds(pl.multiple_of(half * (4 * n) + q * n, n), n)]

    first = []
    for k, (own, full) in enumerate(pairs):
        n = own.shape[0] // 4
        first.append(
            remote(
                own.at[pl.ds(pl.multiple_of(quarter * n, n), n)], rows_at(full, s, quarter),
                send_w.at[k, 0], recv_w.at[k, 0], over_x,
            )
        )
    first[0].start()
    first[1].start()
    locals_ = []
    for k, (src, dst) in enumerate(((tok, tok_all), (cot, cot_all))):
        locals_.append(
            pltpu.make_async_copy(src.at[pl.ds(s * group, group)], dst.at[:, place], local_sem.at[k])
        )
    for k, (own, full) in enumerate(pairs):
        n = own.shape[0]
        locals_.append(
            pltpu.make_async_copy(own, full.at[pl.ds(pl.multiple_of(s * n, n), n)], local_sem.at[2 + k])
        )
    for c in locals_:
        c.start()
    later = []

    def forward(k):
        first[k].wait_recv()
        mine = rows_at(pairs[k][1], o, quarter)
        by_y = remote(mine, mine, send_w.at[k, 1], recv_w.at[k, 1], over_y)
        by_y.start()
        by_core = remote(mine, mine, send_w.at[k, 2], recv_w.at[k, 2], over_core)
        by_core.start()
        later.append((by_y, by_core))

    swaps[1].wait_recv()
    first[2].start()
    forward(0)
    forward(1)
    first[3].start()
    forward(2)
    swaps[2].start()
    forward(3)
    last = []
    for k, (own, full) in enumerate(pairs):
        later[k][0].wait_recv()
        came = rows_at(full, o, flip(quarter, 1))
        c = remote(came, came, send_w.at[k, 3], recv_w.at[k, 3], over_core)
        c.start()
        last.append(c)
    for k in range(4):
        later[k][1].wait_recv()
        last[k].wait_recv()
    for c in (swaps[0], swaps[2]):
        c.wait_recv()
    for c in locals_:
        c.wait()
    for c in swaps + first + last:
        c.wait_send()
    for a, b in later:
        a.wait_send()
        b.wait_send()


def gather_all(tok, cot, small, wa, wo, ww, wn):
    any_spec = pl.BlockSpec(memory_space=pl.ANY)
    group = tok.shape[0] // 2

    def full(w):
        return jax.ShapeDtypeStruct((w.shape[0] * 2, w.shape[1]), w.dtype)

    tokens = jax.ShapeDtypeStruct((group, 2 * tok.shape[1], D), BF16)
    return pl.pallas_call(
        gather_kernel,
        out_shape=(
            tokens, tokens, jax.ShapeDtypeStruct(small.shape, small.dtype),
            full(wa), full(wo), full(ww), full(wn),
        ),
        in_specs=[any_spec] * 7,
        out_specs=(any_spec,) * 7,
        scratch_shapes=[
            pltpu.SemaphoreType.DMA((3,)),
            pltpu.SemaphoreType.DMA((3,)),
            pltpu.SemaphoreType.DMA((4, 4)),
            pltpu.SemaphoreType.DMA((4, 4)),
            pltpu.SemaphoreType.DMA((6,)),
        ],
        compiler_params=pltpu.CompilerParams(collective_id=0, has_side_effects=True),
    )(tok, cot, small, wa, wo, ww, wn)


def reduce_kernel(
    bits, grads, block, out, blocks,
    core_in, x_out, x_in, total, half_out, half_in, extra_out, extra_in,
    send_sem, recv_sem, send_blk, recv_blk, local_sem,
):
    r, s = lax.axis_index("replica"), lax.axis_index("shard")
    o = 1 - s
    over_x = (r, o)
    over = [(flip(r, k), s) for k in range(bits)]
    greet([over_x] + over)
    core = bit_of(r, 0)

    def remote(src, dst, send, recv, device):
        copy = pltpu.make_async_remote_copy(
            src_ref=src, dst_ref=dst, send_sem=send, recv_sem=recv,
            device_id=device, device_id_type=pl.DeviceIdType.MESH,
        )
        copy.start()
        return copy

    pending = []

    order = [(over[k], bit_of(r, k)) for k in range(bits - 1, 0, -1)]
    order += [(over_x, s), (over[0], core)]
    index = sum(b * (1 << k) for k, (_, b) in enumerate(order))
    own_block = pltpu.make_async_copy(block, blocks.at[index], local_sem)
    own_block.start()

    def gather_steps():
        own_block.wait()
        for k, (device, _) in enumerate(order):
            count = 1 << k
            start = (index // count) * count
            part = blocks.at[pl.ds(start, count)]
            c = remote(part, part, send_blk.at[k], recv_blk.at[k], device)
            pending.append(c)
            yield
            c.wait_recv()

    def rows(n, start):
        return pl.ds(pl.multiple_of(start, 16), n)

    def chunk_steps(j):
        base = j * ROWS
        half = ROWS // 2
        away = rows(half, base + (1 - core) * half)
        kept = rows(half, base + core * half)
        c = remote(grads.at[:, away], core_in.at[j], send_sem.at[j, 0], recv_sem.at[j, 0], over[0])
        pending.append(c)
        yield
        c.wait_recv()
        x_out[j] = (grads[o, kept].astype(F32) + core_in[j, o].astype(F32)).astype(BF16)
        c = remote(x_out.at[j], x_in.at[j], send_sem.at[j, 1], recv_sem.at[j, 1], over_x)
        pending.append(c)
        total[j] = grads[s, kept].astype(F32) + core_in[j, s].astype(F32)
        yield
        c.wait_recv()
        total[j] += x_in[j].astype(F32)
        n, start, at = half // 2, 0, 0
        for k in (1, 2, 3):
            b = bit_of(r, k)
            spot = rows(n, at)
            half_out[j, spot] = total[j, rows(n, start + (1 - b) * n)].astype(BF16)
            c = remote(
                half_out.at[j, spot], half_in.at[j, spot],
                send_sem.at[j, 1 + k], recv_sem.at[j, 1 + k], over[k],
            )
            pending.append(c)
            yield
            c.wait_recv()
            start = start + b * n
            total[j, rows(n, start)] += half_in[j, spot].astype(F32)
            at += n
            n //= 2
        n *= 2
        for e in range(bits - 4):
            extra_out[j, e] = total[j, rows(n, start)].astype(BF16)
            c = remote(
                extra_out.at[j, e], extra_in.at[j, e],
                send_sem.at[j, 9 + e], recv_sem.at[j, 9 + e], over[4 + e],
            )
            pending.append(c)
            yield
            c.wait_recv()
            total[j, rows(n, start)] += extra_in[j, e].astype(F32)
        spot = base + core * half + start
        out[rows(n, spot)] = total[j, rows(n, start)].astype(BF16)
        for step, k in enumerate((3, 2, 1, 0)):
            part = out.at[rows(n, spot)]
            c = remote(part, part, send_sem.at[j, 5 + step], recv_sem.at[j, 5 + step], over[k])
            pending.append(c)
            yield
            c.wait_recv()
            spot = spot - bit_of(r, k) * n
            n *= 2

    waiting = [chunk_steps(j) for j in range(CHUNKS)]
    running = [gather_steps()]
    while running or waiting:
        if waiting:
            running.append(waiting.pop(0))
        for steps in list(running):
            if next(steps, 0) == 0:
                running.remove(steps)
    for c in pending:
        c.wait_send()


def reduce_all(grads, block, replicas):
    bits = replicas.bit_length() - 1
    extra = max(bits - 4, 1)
    vmem = pl.BlockSpec(memory_space=pltpu.VMEM)
    half = ROWS // 2
    return pl.pallas_call(
        functools.partial(reduce_kernel, bits),
        out_shape=(
            jax.ShapeDtypeStruct((CHUNKS * ROWS, D), BF16),
            jax.ShapeDtypeStruct((2 * replicas, BLOCK_ROWS, 128), BF16),
        ),
        in_specs=[vmem, vmem],
        out_specs=(vmem, vmem),
        scratch_shapes=[
            pltpu.VMEM((CHUNKS, 2, half, D), BF16),
            pltpu.VMEM((CHUNKS, half, D), BF16),
            pltpu.VMEM((CHUNKS, half, D), BF16),
            pltpu.VMEM((CHUNKS, half, D), F32),
            pltpu.VMEM((CHUNKS, half, D), BF16),
            pltpu.VMEM((CHUNKS, half, D), BF16),
            pltpu.VMEM((CHUNKS, extra, half // 8, D), BF16),
            pltpu.VMEM((CHUNKS, extra, half // 8, D), BF16),
            pltpu.SemaphoreType.DMA((CHUNKS, 9 + extra)),
            pltpu.SemaphoreType.DMA((CHUNKS, 9 + extra)),
            pltpu.SemaphoreType.DMA((bits + 1,)),
            pltpu.SemaphoreType.DMA((bits + 1,)),
            pltpu.SemaphoreType.DMA,
        ],
        compiler_params=pltpu.CompilerParams(
            collective_id=1, has_side_effects=True, vmem_limit_bytes=48 * 2**20
        ),
    )(grads, block)


def dot_nn(a, b):
    return lax.dot_general(a, b, (((1,), (0,)), ((), ())), preferred_element_type=F32)


def dot_nt(a, b):
    return lax.dot_general(a, b, (((1,), (1,)), ((), ())), preferred_element_type=F32)


def dot_tn(a, b):
    return lax.dot_general(a, b, (((0,), (0,)), ((), ())), preferred_element_type=F32)


def row_sum(values):
    return jnp.sum(values, axis=0, keepdims=True)


def normalise(values):
    centered = values - jnp.mean(values, axis=-1, keepdims=True)
    inverse = lax.rsqrt(jnp.mean(centered * centered, axis=-1, keepdims=True) + 1e-06)
    return centered * inverse, inverse


def normalise_back(grad, unit, inverse, scale):
    grad = grad * (1.0 + scale)
    inner = jnp.mean(grad * unit, axis=-1, keepdims=True)
    return inverse * (grad - jnp.mean(grad, axis=-1, keepdims=True) - unit * inner)


def block_kernel(
    tok, cot, mod, b_attend, b_output, b_expand, b_shrink, wa, wo, ww, wn,
    tok_out, grad_tok, d_mod, grads, b_grads,
    n_one, proj, att, n_two, hidden, d_mlp_all, d_pre_all, d_attn_all, d_proj, probs,
):
    step = pl.program_id(0)
    seq = tok.shape[1]
    at = pl.ds(pl.multiple_of(step * seq, seq), seq)
    shift_one, scale_one, gate_one, shift_two, scale_two, gate_two = (
        mod[0, :, i * D : (i + 1) * D] for i in range(6)
    )
    lane = lax.broadcasted_iota(jnp.int32, (1, 2 * HEAD_DIM), 1)
    masks = [
        jnp.where(lane < HEAD_DIM, 1.0, 0.0).astype(BF16),
        jnp.where(lane < HEAD_DIM, 0.0, 1.0).astype(BF16),
    ]
    width = 2 * HEAD_DIM
    score_scale = HEAD_DIM ** (-0.5)

    @pl.when(step == 0)
    def _():
        b_grads[...] = jnp.zeros_like(b_grads)

    def add_bias(start, value):
        b_grads[:, start : start + value.shape[1]] += row_sum(value.astype(F32))

    x = tok[0].astype(F32)
    unit_one, inv_one = normalise(x)
    n_one[at] = (unit_one * (1.0 + scale_one) + shift_one).astype(BF16)
    for i in range(3):
        cols = slice(i * D, (i + 1) * D)
        proj[:, cols] = (dot_nn(n_one[at], wa[:, cols]) + b_attend[:, cols]).astype(BF16)
    for p in range(HEADS // 2):
        cols = slice(p * width, (p + 1) * width)
        query = proj[:, cols]
        key = proj[:, D + p * width : D + (p + 1) * width]
        value = proj[:, 2 * D + p * width : 2 * D + (p + 1) * width]
        total = None
        for h in range(2):
            scores = dot_nt(query, key * masks[h]) * score_scale
            expo = jnp.exp(scores - jnp.max(scores, axis=-1, keepdims=True))
            prob = expo * (1.0 / jnp.sum(expo, axis=-1, keepdims=True))
            probs[2 * p + h] = prob
            part = dot_nn(prob.astype(BF16), value * masks[h])
            total = part if total is None else total + part
        att[at, cols] = total.astype(BF16)
    attn_out = dot_nn(att[at], wo[...]) + b_output[...]
    middle = x + gate_one * attn_out
    unit_two, inv_two = normalise(middle)
    n_two[at] = (unit_two * (1.0 + scale_two) + shift_two).astype(BF16)
    up = cot[0].astype(F32)
    d_mlp = (gate_two * up).astype(BF16)
    d_mlp_all[at] = d_mlp
    add_bias(3 * D + FF, d_mlp)
    mlp = jnp.zeros((seq, D), F32)
    d_two = jnp.zeros((seq, D), F32)
    c0 = (2.0 / jnp.pi) ** 0.5
    for i in range(FF // D):
        cols = slice(i * D, (i + 1) * D)
        pre = dot_nn(n_two[at], ww[:, cols]) + b_expand[:, cols]
        square = pre * pre
        tanh = jnp.tanh(c0 * pre * (1.0 + 0.044715 * square))
        act = (0.5 * pre * (1.0 + tanh)).astype(BF16)
        slope = 0.5 * (1.0 + tanh) + 0.5 * pre * (1.0 - tanh * tanh) * (
            c0 * (1.0 + 3 * 0.044715 * square)
        )
        hidden[at, cols] = act
        mlp += dot_nn(act, wn[cols, :])
        d_pre = (dot_nt(d_mlp, wn[cols, :]) * slope).astype(BF16)
        d_pre_all[at, cols] = d_pre
        add_bias(3 * D + i * D, d_pre)
        d_two += dot_nt(d_pre, ww[:, cols])
    mlp += b_shrink[...]
    tok_out[0] = (middle + gate_two * mlp).astype(BF16)
    d_mod[0, :, 5 * D : 6 * D] = row_sum(up * mlp)
    d_mod[0, :, 3 * D : 4 * D] = row_sum(d_two)
    d_mod[0, :, 4 * D : 5 * D] = row_sum(d_two * unit_two)
    d_middle = up + normalise_back(d_two, unit_two, inv_two, scale_two)
    d_attn = (gate_one * d_middle).astype(BF16)
    d_attn_all[at] = d_attn
    add_bias(2 * D, d_attn)
    d_mod[0, :, 2 * D : 3 * D] = row_sum(d_middle * attn_out)
    d_att = dot_nt(d_attn, wo[...]).astype(BF16)
    for p in range(HEADS // 2):
        cols = slice(p * width, (p + 1) * width)
        query = proj[:, cols]
        key = proj[:, D + p * width : D + (p + 1) * width]
        value = proj[:, 2 * D + p * width : 2 * D + (p + 1) * width]
        grad = d_att[:, cols]
        d_q = d_k = d_v = None
        for h in range(2):
            prob = probs[2 * p + h]
            d_prob = dot_nt(grad, value * masks[h])
            delta = jnp.sum(prob * d_prob, axis=-1, keepdims=True)
            d_score = (prob * (d_prob - delta)).astype(BF16)
            parts = (
                dot_nn(d_score, key * masks[h]),
                dot_tn(d_score, query * masks[h]),
                dot_tn(prob.astype(BF16), grad * masks[h]),
            )
            d_q, d_k, d_v = parts if h == 0 else (d_q + parts[0], d_k + parts[1], d_v + parts[2])
        d_proj[at, cols] = (d_q * score_scale).astype(BF16)
        d_proj[at, D + p * width : D + (p + 1) * width] = (d_k * score_scale).astype(BF16)
        d_proj[at, 2 * D + p * width : 2 * D + (p + 1) * width] = d_v.astype(BF16)
    add_bias(0, d_proj[at, :D])
    add_bias(D, d_proj[at, 2 * D :])
    d_one = dot_nt(d_proj[at], wa[...])
    d_mod[0, :, 0:D] = row_sum(d_one)
    d_mod[0, :, D : 2 * D] = row_sum(d_one * unit_one)
    grad_tok[0] = d_middle + normalise_back(d_one, unit_one, inv_one, scale_one)

    @pl.when(step == pl.num_programs(0) - 1)
    def _():
        half = D // 2
        for i in range(4):
            cols = slice(i * D, (i + 1) * D)
            part = dot_tn(hidden[:, cols], d_mlp_all[...]).astype(BF16)
            grads[i // 2, (i % 2) * D : (i % 2 + 1) * D] = part
            part = dot_tn(n_two[...], d_pre_all[:, cols]).astype(BF16)
            for h in range(2):
                grads[h, 2 * D + i * half : 2 * D + (i + 1) * half] = part[h * half : (h + 1) * half]
        for i in range(3):
            part = dot_tn(n_one[...], d_proj[:, i * D : (i + 1) * D]).astype(BF16)
            for h in range(2):
                grads[h, 4 * D + i * half : 4 * D + (i + 1) * half] = part[h * half : (h + 1) * half]
        part = dot_tn(att[...], d_attn_all[...]).astype(BF16)
        for h in range(2):
            grads[h, 4 * D + 3 * half : 4 * D + 4 * half] = part[h * half : (h + 1) * half]


def block_all(tok, cot, mod, biases, weights):
    latents, seq, _ = tok.shape
    rows = latents * seq
    each = pl.BlockSpec((1, seq, D), lambda i: (i, 0, 0))
    mods = pl.BlockSpec((1, 1, 6 * D), lambda i: (i, 0, 0))

    def whole(shape):
        zeros = (0,) * len(shape)
        return pl.BlockSpec(shape, lambda i: zeros)

    scratch = [(rows, D), (seq, 3 * D), (rows, D), (rows, D), (rows, FF), (rows, D), (rows, FF), (rows, D), (rows, 3 * D)]
    shared = list(biases) + list(weights)
    flops = 2 * 3 * rows * (D * 3 * D + D * D + 2 * D * FF)
    return pl.pallas_call(
        block_kernel,
        grid=(latents,),
        out_shape=(
            jax.ShapeDtypeStruct(tok.shape, BF16),
            jax.ShapeDtypeStruct(tok.shape, F32),
            jax.ShapeDtypeStruct((latents, 1, 6 * D), F32),
            jax.ShapeDtypeStruct((2, CHUNKS * ROWS, D), BF16),
            jax.ShapeDtypeStruct((1, 4 * D + FF), F32),
        ),
        in_specs=[each, each, mods] + [whole(w.shape) for w in shared],
        out_specs=(each, each, mods, whole((2, CHUNKS * ROWS, D)), whole((1, 4 * D + FF))),
        scratch_shapes=[pltpu.VMEM(n, BF16) for n in scratch] + [pltpu.VMEM((HEADS, seq, seq), F32)],
        compiler_params=pltpu.CompilerParams(
            vmem_limit_bytes=56 * 2**20, dimension_semantics=("arbitrary",)
        ),
        cost_estimate=pl.CostEstimate(flops=flops, bytes_accessed=12 * 2**20, transcendentals=rows * FF),
    )(tok, cot, mod, *shared)


def on_device(
    tokens_in,
    condition,
    cotangent,
    modulate_weight,
    modulate_bias,
    attend_weight,
    query_value_bias,
    output_weight,
    output_bias,
    widening_weight,
    widening_bias,
    narrowing_weight,
    narrowing_bias,
):
    rank = lax.axis_index("shard")
    replicas = lax.axis_size("replica")
    latents = tokens_in.shape[0] // 2
    local_len = tokens_in.shape[1]
    own_rows = D // 2
    cond_float = condition.astype(F32)
    cond_act_all = jax.nn.silu(cond_float).astype(BF16)
    own_act = lax.dynamic_slice_in_dim(cond_act_all, rank * own_rows, own_rows, 1)
    mod_part = jnp.dot(own_act, modulate_weight, preferred_element_type=F32)
    mod_keep = lax.dynamic_slice_in_dim(mod_part, rank * latents, latents, 0)
    mod_send = lax.dynamic_slice_in_dim(mod_part, (1 - rank) * latents, latents, 0)
    biases = jnp.concatenate(
        [modulate_bias, query_value_bias, output_bias, widening_bias, narrowing_bias]
    ).astype(F32)
    sent = jnp.concatenate([mod_send.reshape(-1), biases])
    pad = (-sent.shape[0]) % 1024
    small = jnp.pad(sent, (0, pad)).reshape(-1, 128)
    tokens_in, cotangent, small_other, w_attend, w_output, widening_matrix, narrowing_matrix = (
        gather_all(
            tokens_in, cotangent, small, attend_weight, output_weight, widening_weight, narrowing_weight
        )
    )
    small_other = small_other.reshape(-1)
    count = latents * 6 * D
    mod_other = small_other[:count].reshape(latents, 6 * D)
    bias_other = small_other[count : count + biases.shape[0]]

    def both(start, size):
        own, other = biases[start : start + size], bias_other[start : start + size]
        return jnp.where(
            rank == 0, jnp.concatenate([own, other]), jnp.concatenate([other, own])
        )

    b_modulate = both(0, 3 * D)
    b_query_value = both(3 * D, D)
    b_output = both(4 * D, D // 2)
    b_expand = both(4 * D + D // 2, FF // 2)
    b_shrink = both(4 * D + D // 2 + FF // 2, D // 2)

    modulation = mod_keep + mod_other + b_modulate
    full_bias = jnp.concatenate([b_query_value[:D], jnp.zeros((D,), F32), b_query_value[D:]])
    tokens_out, grad_work, d_modulation, grads, bias_all = block_all(
        tokens_in, cotangent, modulation[:, None, :],
        [b[None] for b in (full_bias, b_output, b_expand, b_shrink)],
        (w_attend, w_output, widening_matrix, narrowing_matrix),
    )
    d_modulation = d_modulation[:, 0].astype(BF16)
    bias_all = bias_all[0].astype(BF16)
    return finish(
        rank, replicas, latents, local_len, cond_float, cond_act_all, modulate_weight, tokens_out,
        grad_work, d_modulation, grads, bias_all,
    )


def finish(
    rank, replicas, latents, local_len, cond_float, cond_act_all, modulate_weight, tokens_out,
    grad_work, d_modulation, grads, bias_all,
):
    def in_order(own, other):
        return jnp.where(rank == 0, jnp.concatenate([own, other]), jnp.concatenate([other, own]))

    def give_back(values):
        own = lax.dynamic_slice_in_dim(values, rank * local_len, local_len, 1)
        away = lax.dynamic_slice_in_dim(values, (1 - rank) * local_len, local_len, 1)
        other = lax.ppermute(away.astype(BF16), "shard", SWAP).astype(values.dtype)
        return in_order(own, other)

    own_cond = lax.dynamic_slice_in_dim(cond_act_all, rank * latents, latents, 0)
    flat = jnp.concatenate([d_modulation.reshape(-1), own_cond.reshape(-1), bias_all])
    block = jnp.pad(flat, (0, BLOCK_ROWS * 128 - flat.shape[0])).reshape(BLOCK_ROWS, 128)
    tokens_result = give_back(tokens_out)
    grad_result = give_back(grad_work)
    d_mod_other = lax.ppermute(d_modulation, "shard", SWAP)
    d_cond_part = jnp.einsum(
        "le,de->ld", in_order(d_modulation, d_mod_other), modulate_weight, preferred_element_type=F32
    )
    d_cond_other = lax.ppermute(d_cond_part, "shard", SWAP)
    d_cond = jnp.where(
        rank == 0,
        jnp.concatenate([d_cond_part, d_cond_other], axis=1),
        jnp.concatenate([d_cond_other, d_cond_part], axis=1),
    )
    _, silu_back = jax.vjp(jax.nn.silu, cond_float)
    grad_condition = silu_back(d_cond)[0]

    reduced, blocks = reduce_all(grads, block, replicas)
    flat_blocks = blocks.reshape(2 * replicas, BLOCK_ROWS * 128)
    n_mod, n_cond = latents * 6 * D, latents * D
    d_mod_all = flat_blocks[:, :n_mod].reshape(-1, 6 * D)
    act_all = flat_blocks[:, n_mod : n_mod + n_cond].reshape(-1, D)
    bias_sum = jnp.sum(flat_blocks[:, n_mod + n_cond : n_mod + n_cond + bias_all.shape[0]].astype(F32), axis=0)
    own_act = lax.dynamic_slice_in_dim(act_all, rank * (D // 2), D // 2, 1)
    g_modulate_w = jnp.einsum("lr,le->re", own_act, d_mod_all, preferred_element_type=F32)
    g_modulate_b = jnp.sum(
        lax.dynamic_slice_in_dim(d_mod_all, rank * 3 * D, 3 * D, 1).astype(F32), axis=0
    )

    def own_bias(start, size):
        return lax.dynamic_slice_in_dim(bias_sum, start + rank * (size // 2), size // 2, 0)

    reduced = reduced.astype(F32)
    half = D // 2
    expand = jnp.concatenate([reduced[768 + i * half : 768 + (i + 1) * half] for i in range(4)], axis=1)
    attend = jnp.concatenate([reduced[1536 + i * half : 1536 + (i + 1) * half] for i in range(3)], axis=1)
    return (
        tokens_result,
        grad_result,
        grad_condition,
        g_modulate_w,
        g_modulate_b,
        attend,
        own_bias(0, 2 * D),
        reduced[1536 + 3 * half :],
        own_bias(2 * D, D),
        expand,
        own_bias(3 * D, FF),
        reduced[:768],
        own_bias(3 * D + FF, D),
    )


def solution(mesh):
    specs = (
        P("shard", None),
        P("shard"),
        P("shard", None),
        P("shard"),
        P("shard", None),
        P("shard"),
        P("shard", None),
        P("shard"),
        P("shard", None),
        P("shard"),
    )
    tokens = P("replica", "shard", None)
    return jax.shard_map(
        on_device,
        mesh=mesh,
        in_specs=(tokens, P("replica", None), tokens) + specs,
        out_specs=(tokens, tokens, P("replica", None)) + specs,
        check_vma=False,
    )
```

```python
import functools
import jax
import jax.numpy as jnp
from jax import lax
from jax.experimental import pallas as pl
from jax.experimental.pallas import tpu as pltpu
from jax.sharding import PartitionSpec as P

D = 384
HEADS = 6
HEAD_DIM = 64
FF = 1536
CHUNKS = 3
ROWS = 768
BLOCK_ROWS = 80
F32 = jnp.float32
BF16 = jnp.bfloat16
SWAP = [(0, 1), (1, 0)]


def flip(index, bit):
    step = 1 << bit
    return index + step - 2 * step * ((index // step) % 2)


def bit_of(index, bit):
    return (index // (1 << bit)) % 2


def greet(partners):
    barrier = pltpu.get_barrier_semaphore()
    for partner in partners:
        pl.semaphore_signal(barrier, inc=1, device_id=partner, device_id_type=pl.DeviceIdType.MESH)
    pl.semaphore_wait(barrier, len(partners))


def gather_kernel(
    tok, cot, small, wa, wo, ww, wn,
    tok_all, cot_all, small_other, wa_all, wo_all, ww_all, wn_all,
    send_one, recv_one, send_w, recv_w,
):
    r, s = lax.axis_index("replica"), lax.axis_index("shard")
    o = 1 - s
    over_x, over_core, over_y = (r, o), (flip(r, 0), s), (flip(r, 1), s)
    greet((over_x, over_core, over_y))

    def remote(src, dst, send, recv, device):
        copy = pltpu.make_async_remote_copy(
            src_ref=src, dst_ref=dst, send_sem=send, recv_sem=recv,
            device_id=device, device_id_type=pl.DeviceIdType.MESH,
        )
        return copy

    length = tok.shape[1]
    group = tok.shape[0] // 2
    place = pl.ds(pl.multiple_of(s * length, length), length)

    def exchange(src, dst, k):
        return remote(
            src.at[pl.ds(o * group, group)], dst.at[:, place], send_one.at[k], recv_one.at[k], over_x
        )

    swaps = [
        remote(small, small_other, send_one.at[0], recv_one.at[0], over_x),
        exchange(tok, tok_all, 1),
        exchange(cot, cot_all, 2),
    ]
    swaps[0].start()
    swaps[1].start()

    pairs = ((wa, wa_all), (wo, wo_all), (ww, ww_all), (wn, wn_all))
    quarter = r % 4

    def rows_at(full, half, q):
        n = full.shape[0] // 8
        return full.at[pl.ds(pl.multiple_of(half * (4 * n) + q * n, n), n)]

    first = []
    for k, (own, full) in enumerate(pairs):
        n = own.shape[0] // 4
        first.append(
            remote(
                own.at[pl.ds(pl.multiple_of(quarter * n, n), n)], rows_at(full, s, quarter),
                send_w.at[k, 0], recv_w.at[k, 0], over_x,
            )
        )
    first[0].start()
    first[1].start()
    tok_all[:, place] = tok[pl.ds(s * group, group)]
    cot_all[:, place] = cot[pl.ds(s * group, group)]
    for own, full in pairs:
        n = own.shape[0]
        full[pl.ds(pl.multiple_of(s * n, n), n)] = own[...]
    later = []

    def forward(k):
        first[k].wait_recv()
        mine = rows_at(pairs[k][1], o, quarter)
        by_y = remote(mine, mine, send_w.at[k, 1], recv_w.at[k, 1], over_y)
        by_y.start()
        by_core = remote(mine, mine, send_w.at[k, 2], recv_w.at[k, 2], over_core)
        by_core.start()
        later.append((by_y, by_core))

    swaps[1].wait_recv()
    first[2].start()
    forward(0)
    forward(1)
    first[3].start()
    forward(2)
    swaps[2].start()
    forward(3)
    last = []
    for k, (own, full) in enumerate(pairs):
        later[k][0].wait_recv()
        came = rows_at(full, o, flip(quarter, 1))
        c = remote(came, came, send_w.at[k, 3], recv_w.at[k, 3], over_core)
        c.start()
        last.append(c)
    for k in range(4):
        later[k][1].wait_recv()
        last[k].wait_recv()
    for c in (swaps[0], swaps[2]):
        c.wait_recv()
    for c in swaps + first + last:
        c.wait_send()
    for a, b in later:
        a.wait_send()
        b.wait_send()


def gather_all(tok, cot, small, wa, wo, ww, wn):
    vmem = pl.BlockSpec(memory_space=pltpu.VMEM)
    group = tok.shape[0] // 2

    def full(w):
        return jax.ShapeDtypeStruct((w.shape[0] * 2, w.shape[1]), w.dtype)

    tokens = jax.ShapeDtypeStruct((group, 2 * tok.shape[1], D), BF16)
    return pl.pallas_call(
        gather_kernel,
        out_shape=(
            tokens, tokens, jax.ShapeDtypeStruct(small.shape, small.dtype),
            full(wa), full(wo), full(ww), full(wn),
        ),
        in_specs=[vmem] * 7,
        out_specs=(vmem,) * 7,
        scratch_shapes=[
            pltpu.SemaphoreType.DMA((3,)),
            pltpu.SemaphoreType.DMA((3,)),
            pltpu.SemaphoreType.DMA((4, 4)),
            pltpu.SemaphoreType.DMA((4, 4)),
        ],
        compiler_params=pltpu.CompilerParams(
            collective_id=0, has_side_effects=True, vmem_limit_bytes=48 * 2**20
        ),
    )(tok, cot, small, wa, wo, ww, wn)


def reduce_kernel(
    bits, grads, block, out, blocks,
    core_in, x_out, x_in, total, half_out, half_in, extra_out, extra_in,
    send_sem, recv_sem, send_blk, recv_blk, local_sem,
):
    r, s = lax.axis_index("replica"), lax.axis_index("shard")
    o = 1 - s
    over_x = (r, o)
    over = [(flip(r, k), s) for k in range(bits)]
    greet([over_x] + over)
    core = bit_of(r, 0)

    def remote(src, dst, send, recv, device):
        copy = pltpu.make_async_remote_copy(
            src_ref=src, dst_ref=dst, send_sem=send, recv_sem=recv,
            device_id=device, device_id_type=pl.DeviceIdType.MESH,
        )
        copy.start()
        return copy

    pending = []

    order = [(over[k], bit_of(r, k)) for k in range(bits - 1, 0, -1)]
    order += [(over_x, s), (over[0], core)]
    index = sum(b * (1 << k) for k, (_, b) in enumerate(order))
    own_block = pltpu.make_async_copy(block, blocks.at[index], local_sem)
    own_block.start()

    def gather_steps():
        own_block.wait()
        for k, (device, _) in enumerate(order):
            count = 1 << k
            start = (index // count) * count
            part = blocks.at[pl.ds(start, count)]
            c = remote(part, part, send_blk.at[k], recv_blk.at[k], device)
            pending.append(c)
            yield
            c.wait_recv()

    def rows(n, start):
        return pl.ds(pl.multiple_of(start, 16), n)

    def chunk_steps(j):
        base = j * ROWS
        half = ROWS // 2
        away = rows(half, base + (1 - core) * half)
        kept = rows(half, base + core * half)
        c = remote(grads.at[:, away], core_in.at[j], send_sem.at[j, 0], recv_sem.at[j, 0], over[0])
        pending.append(c)
        yield
        c.wait_recv()
        x_out[j] = (grads[o, kept].astype(F32) + core_in[j, o].astype(F32)).astype(BF16)
        c = remote(x_out.at[j], x_in.at[j], send_sem.at[j, 1], recv_sem.at[j, 1], over_x)
        pending.append(c)
        total[j] = grads[s, kept].astype(F32) + core_in[j, s].astype(F32)
        yield
        c.wait_recv()
        total[j] += x_in[j].astype(F32)
        n, start, at = half // 2, 0, 0
        for k in (1, 2, 3):
            b = bit_of(r, k)
            spot = rows(n, at)
            half_out[j, spot] = total[j, rows(n, start + (1 - b) * n)].astype(BF16)
            c = remote(
                half_out.at[j, spot], half_in.at[j, spot],
                send_sem.at[j, 1 + k], recv_sem.at[j, 1 + k], over[k],
            )
            pending.append(c)
            yield
            c.wait_recv()
            start = start + b * n
            total[j, rows(n, start)] += half_in[j, spot].astype(F32)
            at += n
            n //= 2
        n *= 2
        for e in range(bits - 4):
            extra_out[j, e] = total[j, rows(n, start)].astype(BF16)
            c = remote(
                extra_out.at[j, e], extra_in.at[j, e],
                send_sem.at[j, 9 + e], recv_sem.at[j, 9 + e], over[4 + e],
            )
            pending.append(c)
            yield
            c.wait_recv()
            total[j, rows(n, start)] += extra_in[j, e].astype(F32)
        spot = base + core * half + start
        out[rows(n, spot)] = total[j, rows(n, start)].astype(BF16)
        for step, k in enumerate((3, 2, 1, 0)):
            part = out.at[rows(n, spot)]
            c = remote(part, part, send_sem.at[j, 5 + step], recv_sem.at[j, 5 + step], over[k])
            pending.append(c)
            yield
            c.wait_recv()
            spot = spot - bit_of(r, k) * n
            n *= 2

    chunks = [chunk_steps(j) for j in range(CHUNKS)]
    for steps in chunks:
        next(steps)
    running = [gather_steps()]
    while running or chunks:
        if chunks:
            running.insert(0, chunks.pop(0))
        for steps in list(running):
            if next(steps, 0) == 0:
                running.remove(steps)
    for c in pending:
        c.wait_send()


def reduce_all(grads, block, replicas):
    bits = replicas.bit_length() - 1
    extra = max(bits - 4, 1)
    vmem = pl.BlockSpec(memory_space=pltpu.VMEM)
    half = ROWS // 2
    return pl.pallas_call(
        functools.partial(reduce_kernel, bits),
        out_shape=(
            jax.ShapeDtypeStruct((CHUNKS * ROWS, D), BF16),
            jax.ShapeDtypeStruct((2 * replicas, BLOCK_ROWS, 128), BF16),
        ),
        in_specs=[vmem, vmem],
        out_specs=(vmem, vmem),
        scratch_shapes=[
            pltpu.VMEM((CHUNKS, 2, half, D), BF16),
            pltpu.VMEM((CHUNKS, half, D), BF16),
            pltpu.VMEM((CHUNKS, half, D), BF16),
            pltpu.VMEM((CHUNKS, half, D), F32),
            pltpu.VMEM((CHUNKS, half, D), BF16),
            pltpu.VMEM((CHUNKS, half, D), BF16),
            pltpu.VMEM((CHUNKS, extra, half // 8, D), BF16),
            pltpu.VMEM((CHUNKS, extra, half // 8, D), BF16),
            pltpu.SemaphoreType.DMA((CHUNKS, 9 + extra)),
            pltpu.SemaphoreType.DMA((CHUNKS, 9 + extra)),
            pltpu.SemaphoreType.DMA((bits + 1,)),
            pltpu.SemaphoreType.DMA((bits + 1,)),
            pltpu.SemaphoreType.DMA,
        ],
        compiler_params=pltpu.CompilerParams(
            collective_id=1, has_side_effects=True, vmem_limit_bytes=48 * 2**20
        ),
    )(grads, block)


def dot_nn(a, b):
    return lax.dot_general(a, b, (((1,), (0,)), ((), ())), preferred_element_type=F32)


def dot_nt(a, b):
    return lax.dot_general(a, b, (((1,), (1,)), ((), ())), preferred_element_type=F32)


def dot_tn(a, b):
    return lax.dot_general(a, b, (((0,), (0,)), ((), ())), preferred_element_type=F32)


def row_sum(values):
    return jnp.sum(values, axis=0, keepdims=True)


def normalise(values):
    centered = values - jnp.mean(values, axis=-1, keepdims=True)
    inverse = lax.rsqrt(jnp.mean(centered * centered, axis=-1, keepdims=True) + 1e-06)
    return centered * inverse, inverse


def normalise_back(grad, unit, inverse, scale):
    grad = grad * (1.0 + scale)
    inner = jnp.mean(grad * unit, axis=-1, keepdims=True)
    return inverse * (grad - jnp.mean(grad, axis=-1, keepdims=True) - unit * inner)


def block_kernel(
    tok, cot, mod, b_attend, b_output, b_expand, b_shrink, wa, wo, ww, wn,
    tok_out, grad_tok, d_mod, grads, b_grads,
    n_one, proj, att, n_two, hidden, d_mlp_all, d_pre_all, d_attn_all, d_proj, probs,
):
    step = pl.program_id(0)
    seq = tok.shape[1]
    at = pl.ds(pl.multiple_of(step * seq, seq), seq)
    shift_one, scale_one, gate_one, shift_two, scale_two, gate_two = (
        mod[0, :, i * D : (i + 1) * D] for i in range(6)
    )
    lane = lax.broadcasted_iota(jnp.int32, (1, 2 * HEAD_DIM), 1)
    masks = [
        jnp.where(lane < HEAD_DIM, 1.0, 0.0).astype(BF16),
        jnp.where(lane < HEAD_DIM, 0.0, 1.0).astype(BF16),
    ]
    width = 2 * HEAD_DIM
    score_scale = HEAD_DIM ** (-0.5)

    @pl.when(step == 0)
    def _():
        b_grads[...] = jnp.zeros_like(b_grads)

    def add_bias(start, value):
        b_grads[:, start : start + value.shape[1]] += row_sum(value.astype(F32))

    x = tok[0].astype(F32)
    unit_one, inv_one = normalise(x)
    n_one[at] = (unit_one * (1.0 + scale_one) + shift_one).astype(BF16)
    for i in range(3):
        cols = slice(i * D, (i + 1) * D)
        proj[:, cols] = (dot_nn(n_one[at], wa[:, cols]) + b_attend[:, cols]).astype(BF16)
    for p in range(HEADS // 2):
        cols = slice(p * width, (p + 1) * width)
        query = proj[:, cols]
        key = proj[:, D + p * width : D + (p + 1) * width]
        value = proj[:, 2 * D + p * width : 2 * D + (p + 1) * width]
        total = None
        for h in range(2):
            scores = dot_nt(query, key * masks[h]) * score_scale
            expo = jnp.exp(scores - jnp.max(scores, axis=-1, keepdims=True))
            prob = expo * (1.0 / jnp.sum(expo, axis=-1, keepdims=True))
            probs[2 * p + h] = prob
            part = dot_nn(prob.astype(BF16), value * masks[h])
            total = part if total is None else total + part
        att[at, cols] = total.astype(BF16)
    attn_out = dot_nn(att[at], wo[...]) + b_output[...]
    middle = x + gate_one * attn_out
    unit_two, inv_two = normalise(middle)
    n_two[at] = (unit_two * (1.0 + scale_two) + shift_two).astype(BF16)
    up = cot[0].astype(F32)
    d_mlp = (gate_two * up).astype(BF16)
    d_mlp_all[at] = d_mlp
    add_bias(3 * D + FF, d_mlp)
    mlp = jnp.zeros((seq, D), F32)
    d_two = jnp.zeros((seq, D), F32)
    c0 = (2.0 / jnp.pi) ** 0.5
    for i in range(FF // D):
        cols = slice(i * D, (i + 1) * D)
        pre = dot_nn(n_two[at], ww[:, cols]) + b_expand[:, cols]
        square = pre * pre
        tanh = jnp.tanh(c0 * pre * (1.0 + 0.044715 * square))
        act = (0.5 * pre * (1.0 + tanh)).astype(BF16)
        slope = 0.5 * (1.0 + tanh) + 0.5 * pre * (1.0 - tanh * tanh) * (
            c0 * (1.0 + 3 * 0.044715 * square)
        )
        hidden[at, cols] = act
        mlp += dot_nn(act, wn[cols, :])
        d_pre = (dot_nt(d_mlp, wn[cols, :]) * slope).astype(BF16)
        d_pre_all[at, cols] = d_pre
        add_bias(3 * D + i * D, d_pre)
        d_two += dot_nt(d_pre, ww[:, cols])
    mlp += b_shrink[...]
    tok_out[0] = (middle + gate_two * mlp).astype(BF16)
    d_mod[0, :, 5 * D : 6 * D] = row_sum(up * mlp)
    d_mod[0, :, 3 * D : 4 * D] = row_sum(d_two)
    d_mod[0, :, 4 * D : 5 * D] = row_sum(d_two * unit_two)
    d_middle = up + normalise_back(d_two, unit_two, inv_two, scale_two)
    d_attn = (gate_one * d_middle).astype(BF16)
    d_attn_all[at] = d_attn
    add_bias(2 * D, d_attn)
    d_mod[0, :, 2 * D : 3 * D] = row_sum(d_middle * attn_out)
    d_att = dot_nt(d_attn, wo[...]).astype(BF16)
    for p in range(HEADS // 2):
        cols = slice(p * width, (p + 1) * width)
        query = proj[:, cols]
        key = proj[:, D + p * width : D + (p + 1) * width]
        value = proj[:, 2 * D + p * width : 2 * D + (p + 1) * width]
        grad = d_att[:, cols]
        d_q = d_k = d_v = None
        for h in range(2):
            prob = probs[2 * p + h]
            d_prob = dot_nt(grad, value * masks[h])
            delta = jnp.sum(prob * d_prob, axis=-1, keepdims=True)
            d_score = (prob * (d_prob - delta)).astype(BF16)
            parts = (
                dot_nn(d_score, key * masks[h]),
                dot_tn(d_score, query * masks[h]),
                dot_tn(prob.astype(BF16), grad * masks[h]),
            )
            d_q, d_k, d_v = parts if h == 0 else (d_q + parts[0], d_k + parts[1], d_v + parts[2])
        d_proj[at, cols] = (d_q * score_scale).astype(BF16)
        d_proj[at, D + p * width : D + (p + 1) * width] = (d_k * score_scale).astype(BF16)
        d_proj[at, 2 * D + p * width : 2 * D + (p + 1) * width] = d_v.astype(BF16)
    add_bias(0, d_proj[at, :D])
    add_bias(D, d_proj[at, 2 * D :])
    d_one = dot_nt(d_proj[at], wa[...])
    d_mod[0, :, 0:D] = row_sum(d_one)
    d_mod[0, :, D : 2 * D] = row_sum(d_one * unit_one)
    grad_tok[0] = d_middle + normalise_back(d_one, unit_one, inv_one, scale_one)

    @pl.when(step == pl.num_programs(0) - 1)
    def _():
        half = D // 2
        for i in range(4):
            cols = slice(i * D, (i + 1) * D)
            part = dot_tn(hidden[:, cols], d_mlp_all[...]).astype(BF16)
            grads[i // 2, (i % 2) * D : (i % 2 + 1) * D] = part
            part = dot_tn(n_two[...], d_pre_all[:, cols]).astype(BF16)
            for h in range(2):
                grads[h, 2 * D + i * half : 2 * D + (i + 1) * half] = part[h * half : (h + 1) * half]
        for i in range(3):
            part = dot_tn(n_one[...], d_proj[:, i * D : (i + 1) * D]).astype(BF16)
            for h in range(2):
                grads[h, 4 * D + i * half : 4 * D + (i + 1) * half] = part[h * half : (h + 1) * half]
        part = dot_tn(att[...], d_attn_all[...]).astype(BF16)
        for h in range(2):
            grads[h, 4 * D + 3 * half : 4 * D + 4 * half] = part[h * half : (h + 1) * half]


def block_all(tok, cot, mod, biases, weights):
    latents, seq, _ = tok.shape
    rows = latents * seq
    each = pl.BlockSpec((1, seq, D), lambda i: (i, 0, 0))
    mods = pl.BlockSpec((1, 1, 6 * D), lambda i: (i, 0, 0))

    def whole(shape):
        zeros = (0,) * len(shape)
        return pl.BlockSpec(shape, lambda i: zeros)

    scratch = [(rows, D), (seq, 3 * D), (rows, D), (rows, D), (rows, FF), (rows, D), (rows, FF), (rows, D), (rows, 3 * D)]
    shared = list(biases) + list(weights)
    flops = 2 * 3 * rows * (D * 3 * D + D * D + 2 * D * FF)
    return pl.pallas_call(
        block_kernel,
        grid=(latents,),
        out_shape=(
            jax.ShapeDtypeStruct(tok.shape, BF16),
            jax.ShapeDtypeStruct(tok.shape, F32),
            jax.ShapeDtypeStruct((latents, 1, 6 * D), F32),
            jax.ShapeDtypeStruct((2, CHUNKS * ROWS, D), BF16),
            jax.ShapeDtypeStruct((1, 4 * D + FF), F32),
        ),
        in_specs=[each, each, mods] + [whole(w.shape) for w in shared],
        out_specs=(each, each, mods, whole((2, CHUNKS * ROWS, D)), whole((1, 4 * D + FF))),
        scratch_shapes=[pltpu.VMEM(n, BF16) for n in scratch] + [pltpu.VMEM((HEADS, seq, seq), F32)],
        compiler_params=pltpu.CompilerParams(
            vmem_limit_bytes=56 * 2**20, dimension_semantics=("arbitrary",)
        ),
        cost_estimate=pl.CostEstimate(flops=flops, bytes_accessed=12 * 2**20, transcendentals=rows * FF),
    )(tok, cot, mod, *shared)


def unpack_kernel(
    latents, reduced, blocks, g_mod_w, g_mod_b, attend, g_qv, g_out_w, g_out_b, expand, g_exp_b, shrink,
    g_shr_b, wide,
):
    first = lax.axis_index("shard") == 0
    half = D // 2
    wide[...] = blocks[...].astype(F32)
    shrink[...] = reduced[0:ROWS].astype(F32)
    for i in range(4):
        expand[:, i * D : (i + 1) * D] = reduced[ROWS + i * half : ROWS + (i + 1) * half].astype(F32)
    for i in range(3):
        attend[:, i * D : (i + 1) * D] = reduced[
            2 * ROWS + i * half : 2 * ROWS + (i + 1) * half
        ].astype(F32)
    g_out_w[...] = reduced[2 * ROWS + 3 * half :].astype(F32)

    def lines(start, count):
        return jnp.concatenate([wide[:, i, :] for i in range(start, start + count)], axis=1)

    n_mod, n_act = 6 * D // 128, D // 128
    mods = jnp.concatenate([lines(k * n_mod, n_mod) for k in range(latents)], axis=0)
    acts = jnp.concatenate(
        [lines(latents * n_mod + k * n_act, n_act) for k in range(latents)], axis=0
    )
    own = jnp.where(first, acts[:, :half], acts[:, half:]).astype(BF16)
    low = mods.astype(BF16)
    for i in range(6):
        cols = slice(i * D, (i + 1) * D)
        g_mod_w[:, cols] = dot_tn(own, low[:, cols])
    sums = row_sum(mods)
    g_mod_b[...] = jnp.where(first, sums[:, : 3 * D], sums[:, 3 * D :])
    bias = row_sum(lines(latents * (n_mod + n_act), (4 * D + FF) // 128))
    start = 0
    for ref in (g_qv, g_out_b, g_exp_b, g_shr_b):
        n = ref.shape[1]
        ref[...] = jnp.where(first, bias[:, start : start + n], bias[:, start + n : start + 2 * n])
        start += 2 * n


def unpack_all(reduced, blocks, latents):
    vmem = pl.BlockSpec(memory_space=pltpu.VMEM)
    half = D // 2
    shapes = [
        (half, 6 * D), (1, 3 * D), (half, 3 * D), (1, D), (half, D), (1, half), (half, FF), (1, FF // 2),
        (FF // 2, D), (1, half),
    ]
    return pl.pallas_call(
        functools.partial(unpack_kernel, latents),
        out_shape=[jax.ShapeDtypeStruct(n, F32) for n in shapes],
        in_specs=[vmem, vmem],
        out_specs=[vmem] * len(shapes),
        scratch_shapes=[pltpu.VMEM(blocks.shape, F32)],
        compiler_params=pltpu.CompilerParams(vmem_limit_bytes=56 * 2**20),
        cost_estimate=pl.CostEstimate(flops=2**26, bytes_accessed=8 * 2**20, transcendentals=0),
    )(reduced, blocks)


def on_device(
    tokens_in,
    condition,
    cotangent,
    modulate_weight,
    modulate_bias,
    attend_weight,
    query_value_bias,
    output_weight,
    output_bias,
    widening_weight,
    widening_bias,
    narrowing_weight,
    narrowing_bias,
):
    rank = lax.axis_index("shard")
    replicas = lax.axis_size("replica")
    latents = tokens_in.shape[0] // 2
    local_len = tokens_in.shape[1]
    own_rows = D // 2
    cond_float = condition.astype(F32)
    cond_act_all = jax.nn.silu(cond_float).astype(BF16)
    own_act = lax.dynamic_slice_in_dim(cond_act_all, rank * own_rows, own_rows, 1)
    mod_part = jnp.dot(own_act, modulate_weight, preferred_element_type=F32)
    mod_keep = lax.dynamic_slice_in_dim(mod_part, rank * latents, latents, 0)
    mod_send = lax.dynamic_slice_in_dim(mod_part, (1 - rank) * latents, latents, 0)
    biases = jnp.concatenate(
        [modulate_bias, query_value_bias, output_bias, widening_bias, narrowing_bias]
    ).astype(F32)
    sent = jnp.concatenate([mod_send.reshape(-1), biases])
    pad = (-sent.shape[0]) % 1024
    small = jnp.pad(sent, (0, pad)).reshape(-1, 128)
    tokens_in, cotangent, small_other, w_attend, w_output, widening_matrix, narrowing_matrix = (
        gather_all(
            tokens_in, cotangent, small, attend_weight, output_weight, widening_weight, narrowing_weight
        )
    )
    small_other = small_other.reshape(-1)
    count = latents * 6 * D
    mod_other = small_other[:count].reshape(latents, 6 * D)
    bias_other = small_other[count : count + biases.shape[0]]

    def both(start, size):
        own, other = biases[start : start + size], bias_other[start : start + size]
        return jnp.where(
            rank == 0, jnp.concatenate([own, other]), jnp.concatenate([other, own])
        )

    b_modulate = both(0, 3 * D)
    b_query_value = both(3 * D, D)
    b_output = both(4 * D, D // 2)
    b_expand = both(4 * D + D // 2, FF // 2)
    b_shrink = both(4 * D + D // 2 + FF // 2, D // 2)

    modulation = mod_keep + mod_other + b_modulate
    full_bias = jnp.concatenate([b_query_value[:D], jnp.zeros((D,), F32), b_query_value[D:]])
    tokens_out, grad_work, d_modulation, grads, bias_all = block_all(
        tokens_in, cotangent, modulation[:, None, :],
        [b[None] for b in (full_bias, b_output, b_expand, b_shrink)],
        (w_attend, w_output, widening_matrix, narrowing_matrix),
    )
    d_modulation = d_modulation[:, 0].astype(BF16)
    bias_all = bias_all[0].astype(BF16)
    return finish(
        rank, replicas, latents, local_len, cond_float, cond_act_all, modulate_weight, tokens_out,
        grad_work, d_modulation, grads, bias_all,
    )


def finish(
    rank, replicas, latents, local_len, cond_float, cond_act_all, modulate_weight, tokens_out,
    grad_work, d_modulation, grads, bias_all,
):
    def in_order(own, other):
        return jnp.where(rank == 0, jnp.concatenate([own, other]), jnp.concatenate([other, own]))

    def give_back(values):
        own = lax.dynamic_slice_in_dim(values, rank * local_len, local_len, 1)
        away = lax.dynamic_slice_in_dim(values, (1 - rank) * local_len, local_len, 1)
        other = lax.ppermute(away.astype(BF16), "shard", SWAP).astype(values.dtype)
        return in_order(own, other)

    own_cond = lax.dynamic_slice_in_dim(cond_act_all, rank * latents, latents, 0)
    flat = jnp.concatenate([d_modulation.reshape(-1), own_cond.reshape(-1), bias_all])
    block = jnp.pad(flat, (0, BLOCK_ROWS * 128 - flat.shape[0])).reshape(BLOCK_ROWS, 128)
    tokens_result = give_back(tokens_out)
    grad_result = give_back(grad_work)
    d_mod_other = lax.ppermute(d_modulation, "shard", SWAP)
    d_cond_part = jnp.einsum(
        "le,de->ld", in_order(d_modulation, d_mod_other), modulate_weight, preferred_element_type=F32
    )
    d_cond_other = lax.ppermute(d_cond_part, "shard", SWAP)
    d_cond = jnp.where(
        rank == 0,
        jnp.concatenate([d_cond_part, d_cond_other], axis=1),
        jnp.concatenate([d_cond_other, d_cond_part], axis=1),
    )
    _, silu_back = jax.vjp(jax.nn.silu, cond_float)
    grad_condition = silu_back(d_cond)[0]

    reduced, blocks = reduce_all(grads, block, replicas)
    g_mod_w, g_mod_b, attend, g_qv, g_out_w, g_out_b, expand, g_exp_b, shrink, g_shr_b = unpack_all(
        reduced, blocks, latents
    )
    return (
        tokens_result,
        grad_result,
        grad_condition,
        g_mod_w,
        g_mod_b[0],
        attend,
        g_qv[0],
        g_out_w,
        g_out_b[0],
        expand,
        g_exp_b[0],
        shrink,
        g_shr_b[0],
    )


def solution(mesh):
    specs = (
        P("shard", None),
        P("shard"),
        P("shard", None),
        P("shard"),
        P("shard", None),
        P("shard"),
        P("shard", None),
        P("shard"),
        P("shard", None),
        P("shard"),
    )
    tokens = P("replica", "shard", None)
    return jax.shard_map(
        on_device,
        mesh=mesh,
        in_specs=(tokens, P("replica", None), tokens) + specs,
        out_specs=(tokens, tokens, P("replica", None)) + specs,
        check_vma=False,
    )
```
